128 devices in a mesh: blk: 64 (over z, y, x_lo, core), rep: 2 (over x_hi).
Axes of the slice: x: 4 (x_hi: 2, x_lo: 2; x = x_hi * 2 + x_lo), y: 4, z: 4, core: 2. Of those that a mesh axis runs over, the one named last changes fastest.
Arguments:
- examples: float32 [32768, 1024], P(('blk', 'rep')), may hold values from -6 to 6
- targets: float32 [32768, 1000], P(('blk', 'rep')), may hold values from -6 to 6
- hop_reach: int32 [32768], P(('blk', 'rep')), may hold values from 1 to 5
- centers: float32 [16384, 1024], P('blk'), may hold values from -6 to 6
- coeffs: float32 [16384, 1000], P('blk'), may hold values from -0.15625 to 0.15625
- step_gain: float32 [16384], P('blk'), may hold values from 0.5 to 2
Outputs:
- new_coeffs: float32 [16384, 1000], P('blk')
- residual: float32 [32768, 1000], P(('blk', 'rep'))
The draws below stay inside these ranges and needn't reach their ends.
All inputs are finite; a program needn't handle non-finite values.
Results may differ from the reference program's by a relative error of at most 0.0003.
Values sent between devices are 32-bit elements; how exact they have to be, the bound alone decides.
A program may use at most 64 MiB of HBM per device.

```python
import math
import jax
import jax.numpy as jnp
from jax import lax

D = 1024
OUT = 1000
CB = 256
HOPS = 4
EX_DEV = 256
EXAMPLES = 32768
CENTERS = 16384
N_BLK = 64
N_REP = 2


def place_ends(drawn, rng, low, high):
    place = [jax.random.randint(jax.random.fold_in(rng, axis), (), 0, length) for axis, length in enumerate(drawn.shape)]
    longest = drawn.shape.index(max(drawn.shape))
    neighbour = place[:longest] + [(place[longest] + 1) % drawn.shape[longest]] + place[longest + 1:]
    return drawn.at[tuple(place)].set(low).at[tuple(neighbour)].set(high)


def block_levels(stream_key, shape, shards, least, high):
    loudness, own = 1.0, jax.random.fold_in(stream_key, 6)
    for position, parts in shards:
        steps = jnp.exp(jax.random.uniform(jax.random.fold_in(own, position), (parts,), jnp.float32, least / len(shards), high / len(shards)))
        loudness = loudness * jnp.repeat(steps, shape[position] // parts).reshape([-1 if axis == position else 1 for axis in range(len(shape))])
    return loudness


def gaussian(key, dims, deviation, limit, cuts=(), dtype=jnp.bfloat16):
    entries = jax.random.normal(key, dims, jnp.float32) * deviation
    if len(cuts) > 0:
        entries = block_levels(key, dims, cuts, -0.22, 0.18) * entries
    return jnp.clip(entries, min=-limit, max=limit).astype(dtype)


def setup_inputs(seed: int = 0) -> dict:
    key_list = jax.random.split(jax.random.key(seed), 7)
    return {
        "examples": gaussian(key_list[0], (EXAMPLES, D), 1.0, 6.0, ((0, 128),), jnp.float32),
        "targets": gaussian(key_list[1], (EXAMPLES, OUT), 1.0, 6.0, ((0, 128),), jnp.float32),
        "hop_reach": place_ends(jax.random.randint(key_list[2], (EXAMPLES,), 1, HOPS + 2), jax.random.fold_in(key_list[2], 1), 1, (HOPS + 2) - 1).astype(jnp.int32),
        "centers": gaussian(key_list[3], (CENTERS, D), 1.0, 6.0, ((0, 64),), jnp.float32),
        "coeffs": gaussian(key_list[4], (CENTERS, OUT), (CB * (HOPS + 1)) ** -0.5, 0.15625, ((0, 64),), jnp.float32),
        "step_gain": jnp.clip(jnp.exp(math.log(2.0) - 1.3862944 * jax.random.uniform(key_list[5], (CENTERS,), jnp.float32) ** block_levels(key_list[5], (CENTERS,), ((0, 64),), -0.2, 0.2)), 0.5, 2.0),
    }


def reference(examples, targets, hop_reach, centers, coeffs, step_gain):
    rows = N_REP * EX_DEV
    grouped = examples.reshape(N_BLK, rows, D)
    wanted = targets.reshape(N_BLK, rows, OUT)
    reaches = hop_reach.reshape(N_BLK, rows)
    center_blocks = centers.reshape(N_BLK, CB, D)
    coeff_blocks = coeffs.reshape(N_BLK, CB, OUT)
    sharpness = 0.5 / math.sqrt(D)
    kernels = []
    predicted = jnp.zeros((N_BLK, rows, OUT), jnp.float32)
    for distance in range(HOPS + 1):
        seen_centers = jnp.roll(center_blocks, distance, axis=0)
        seen_coeffs = jnp.roll(coeff_blocks, distance, axis=0)
        scores = jnp.einsum('brd,bcd->brc', grouped, seen_centers, precision=lax.Precision.HIGHEST)
        visible = (reaches > distance).astype(jnp.float32)[:, :, None]
        kernel = jnp.exp(sharpness * scores) * visible
        kernels.append(kernel)
        predicted = predicted + jnp.einsum('brc,bco->bro', kernel, seen_coeffs, precision=lax.Precision.HIGHEST)
    residual = predicted - wanted
    gradient = jnp.zeros((N_BLK, CB, OUT), jnp.float32)
    for distance in range(HOPS + 1):
        term = jnp.einsum('brc,bro->bco', kernels[distance], residual, precision=lax.Precision.HIGHEST)
        gradient = gradient + jnp.roll(term, -distance, axis=0)
    step_size = 1.0 / math.sqrt(EX_DEV * N_REP * (HOPS + 1))
    new_coeffs = coeffs - (step_size * step_gain)[:, None] * gradient.reshape(CENTERS, OUT)
    return (new_coeffs, residual.reshape(EXAMPLES, OUT))
```

```python
import functools
import math

import jax
import jax.numpy as jnp
from jax import lax
from jax.experimental import pallas as pl
from jax.experimental.pallas import tpu as pltpu
from jax.sharding import PartitionSpec as P

HOPS = 4
MESH = pl.DeviceIdType.MESH
HIGHEST = lax.Precision.HIGHEST
OWN, D, X, PY, PX = range(5)
NT = (((1,), (1,)), ((), ()))
NN = (((1,), (0,)), ((), ()))


def spans(sizes):
    out, at = [], 0
    for size in sizes:
        out.append((at, size))
        at += size
    return out


def kernel(
    cpieces, wpieces, sharpness,
    ex_hbm, tgt_hbm, hop_ref, cen_hbm, cof_hbm, scale_ref,
    newc_hbm, res_hbm,
    cbuf, wbuf, ex, tgt, kt, res, grad, gsend, rpy, rpx, rx, ry, re, newc,
    d_s, d_r, xa_s, xa_r, xb_s, xb_r, py_s, py_r, px_s, px_r,
    gpy_s, gpy_r, gpx_s, gpx_r, gx_s, gx_r, gy_s, gy_r, ge_s, ge_r,
    load_sem, out_sem,
):
    b = lax.axis_index("blk")
    r = lax.axis_index("rep")
    n_blk = lax.axis_size("blk")
    q = lax.rem(b, 4)
    xl = q // 2
    core = lax.rem(q, 2)
    base = b - q
    is_l = xl == 0
    is_h = xl == 1
    up = (lax.rem(b + 4, n_blk), r)
    down = (lax.rem(b + n_blk - 4, n_blk), r)
    near = base + (1 - xl) * 2 + core
    x1 = (near, r)
    x3 = (near, 1 - r)
    x2 = (b, 1 - r)
    peer = (base + xl * 2 + 1 - core, r)

    def load(i, src, dst):
        return pltpu.make_async_copy(src, dst, load_sem.at[i])

    loads = [
        load(0, cen_hbm, cbuf.at[OWN]),
        load(1, cof_hbm, wbuf.at[OWN]),
        load(2, ex_hbm, ex),
        load(3, tgt_hbm, tgt),
    ]
    for copy in loads:
        copy.start()

    barrier = pltpu.get_barrier_semaphore()
    for other in (up, down, x1, x3, x2, peer):
        pl.semaphore_signal(barrier, inc=1, device_id=other, device_id_type=MESH)
    pl.semaphore_wait(barrier, 6)

    nc, nw = len(cpieces), len(wpieces)
    n = nc + nw

    def part(i, slot):
        if i < nc:
            lo, size = cpieces[i]
            return cbuf.at[slot, pl.ds(lo, size)]
        lo, size = wpieces[i - nc]
        return wbuf.at[slot, pl.ds(lo, size)]

    def cut(i):
        if i < nc:
            lo, size = cpieces[i]
            return cbuf, lo, size // 2, size
        lo, size = wpieces[i - nc]
        return wbuf, lo, 0, size

    def remote(src, dst, ssem, rsem, to):
        return pltpu.make_async_remote_copy(
            src_ref=src, dst_ref=dst, send_sem=ssem, recv_sem=rsem,
            device_id=to, device_id_type=MESH,
        )

    def d_copy(i):
        return remote(part(i, OWN), part(i, D), d_s.at[i], d_r.at[i], up)

    def x_copies(i):
        buf, lo, near_rows, size = cut(i)
        out = []
        if near_rows:
            span = pl.ds(lo, near_rows)
            out.append(remote(buf.at[xl, span], buf.at[X, span], xa_s.at[i], xa_r.at[i], x1))
        span = pl.ds(lo + near_rows, size - near_rows)
        out.append(remote(buf.at[xl, span], buf.at[X, span], xb_s.at[i], xb_r.at[i], x3))
        return out

    def py_copy(i):
        return remote(part(i, core), part(i, PY), py_s.at[i], py_r.at[i], peer)

    def px_copy(i):
        return remote(part(i, X), part(i, PX), px_s.at[i], px_r.at[i], peer)

    def rows(j):
        lo, size = wpieces[j]
        return pl.ds(lo, size)

    def gpy_copy(j):
        return remote(gsend.at[0, rows(j)], rpy.at[rows(j)], gpy_s.at[j], gpy_r.at[j], peer)

    def gpx_copy(j):
        return remote(gsend.at[1, rows(j)], rpx.at[rows(j)], gpx_s.at[j], gpx_r.at[j], peer)

    def gx_copy(j):
        return remote(grad.at[X, rows(j)], rx.at[rows(j)], gx_s.at[j], gx_r.at[j], x1)

    def gy_copy(j):
        return remote(grad.at[D, rows(j)], ry.at[rows(j)], gy_s.at[j], gy_r.at[j], down)

    def ge_copy(j):
        return remote(grad.at[OWN, rows(j)], re.at[rows(j)], ge_s.at[j], ge_r.at[j], x2)

    hop_of = {OWN: 0, D: 4, X: 2, PY: 3 - 2 * core, PX: 1 + 2 * core}

    def scores(slot, lo, size):
        products = lax.dot_general(
            cbuf[slot, lo:lo + size, :], ex[...], NT,
            precision=HIGHEST, preferred_element_type=jnp.float32,
        )
        visible = (hop_ref[...] > hop_of[slot]).astype(jnp.float32)
        kt[slot, lo:lo + size, :] = jnp.exp(sharpness * products) * visible

    def arrive(i):
        d_copy(i).wait_recv()

        @pl.when(is_h)
        def _():
            for copy in x_copies(i):
                copy.start()

        @pl.when(core == 1)
        def _():
            py_copy(i).start()

        d_copy(i).wait_send()
        if i + 2 < n:
            d_copy(i + 2).start()
        if i + nc < n:
            @pl.when(is_l)
            def _():
                for copy in x_copies(i + nc):
                    copy.start()

    def spread(i):
        for copy in x_copies(i):
            copy.wait_recv()
        px_copy(i).start()

    def ready(i):
        py_copy(i).wait_recv()
        px_copy(i).wait_recv()

    def contract(j):
        ready(nc + j)
        lo, size = wpieces[j]
        hi = lo + size
        total = -tgt[lo:hi, :]
        for slot in (OWN, D, X, PY, PX):
            total = total + lax.dot_general(
                wbuf[slot, lo:hi, :], kt[slot], NN,
                precision=HIGHEST, preferred_element_type=jnp.float32,
            )
        res[lo:hi, :] = total

        def term(slot):
            return lax.dot_general(
                res[lo:hi, :], kt[slot], NT,
                precision=HIGHEST, preferred_element_type=jnp.float32,
            )

        gsend[1, lo:hi, :] = term(PX)
        gpx_copy(j).start()
        gsend[0, lo:hi, :] = term(PY)
        gpy_copy(j).start()
        for slot in (X, D, OWN):
            grad[slot, lo:hi, :] = term(slot)
        out_copy(0, j).start()

    def out_copy(which, j):
        src, dst = ((res, res_hbm), (newc, newc_hbm))[which]
        return pltpu.make_async_copy(src.at[rows(j)], dst.at[rows(j)], out_sem.at[which, j])

    def fold(j):
        lo, size = wpieces[j]
        hi = lo + size
        gpx_copy(j).wait_recv()
        grad[X, lo:hi, :] = grad[X, lo:hi, :] + rpx[lo:hi, :]
        gx_copy(j).start()
        gpy_copy(j).wait_recv()

        @pl.when(core == 0)
        def _():
            grad[OWN, lo:hi, :] = grad[OWN, lo:hi, :] + rpy[lo:hi, :]

        @pl.when(core == 1)
        def _():
            grad[D, lo:hi, :] = grad[D, lo:hi, :] + rpy[lo:hi, :]

        @pl.when(is_l)
        def _():
            gy_copy(j).start()

    def descend(j):
        lo, size = wpieces[j]
        hi = lo + size
        gx_copy(j).wait_recv()

        @pl.when(is_h)
        def _():
            grad[D, lo:hi, :] = grad[D, lo:hi, :] + rx[lo:hi, :]
            gy_copy(j).start()

        @pl.when(is_l)
        def _():
            grad[OWN, lo:hi, :] = grad[OWN, lo:hi, :] + rx[lo:hi, :]

    def home(j):
        lo, size = wpieces[j]
        hi = lo + size
        gy_copy(j).wait_recv()
        grad[OWN, lo:hi, :] = grad[OWN, lo:hi, :] + ry[lo:hi, :]
        ge_copy(j).start()

    def finish(j):
        lo, size = wpieces[j]
        hi = lo + size
        ge_copy(j).wait_recv()
        total = grad[OWN, lo:hi, :] + re[lo:hi, :]
        newc[lo:hi, :] = wbuf[OWN, lo:hi, :] - scale_ref[...] * total
        out_copy(1, j).start()

    loads[0].wait()
    d_copy(0).start()
    d_copy(1).start()

    @pl.when(is_l)
    def _():
        for i in range(nc):
            for copy in x_copies(i):
                copy.start()

    loads[1].wait()

    @pl.when(core == 0)
    def _():
        for i in range(n):
            py_copy(i).start()

    loads[2].wait()
    scores(OWN, 0, cbuf.shape[1])
    loads[3].wait()

    def in_range(j):
        return 0 <= j < nw

    for k in range(n + 6):
        if k < n:
            arrive(k)
        if k < nc:
            scores(D, *cpieces[k])
        if 0 <= k - 1 < n:
            spread(k - 1)
        j = k - nc
        if in_range(j - 5):
            finish(j - 5)
        if in_range(j - 4):
            home(j - 4)
        if in_range(j - 3):
            descend(j - 3)
        if in_range(j - 2):
            fold(j - 2)
        if 0 <= k - 1 < nc:
            i = k - 1
            ready(i)
            for slot in (X, PY, PX):
                scores(slot, *cpieces[i])
        if in_range(j - 1):
            contract(j - 1)

    for i in range(n):
        for copy in x_copies(i):
            copy.wait_send()
        py_copy(i).wait_send()
        px_copy(i).wait_send()
    for j in range(nw):
        for make in (gpy_copy, gpx_copy, gx_copy, gy_copy, ge_copy):
            make(j).wait_send()
        out_copy(0, j).wait()
        out_copy(1, j).wait()


def on_device(examples, targets, hop_reach, centers, coeffs, step_gain):
    n_ex, width = examples.shape
    n_cen, n_out = coeffs.shape
    sharpness = 0.5 / math.sqrt(width)
    step_size = 1.0 / math.sqrt(n_ex * lax.axis_size("rep") * (HOPS + 1))
    cpieces = spans([n_cen // 4] * 4)
    wpieces = spans([n_out // 5] * 5)
    nc, nw = len(cpieces), len(wpieces)
    n = nc + nw
    f32 = jnp.float32
    whole = pl.BlockSpec(memory_space=pl.ANY)
    vmem = pl.BlockSpec(memory_space=pltpu.VMEM)
    dma = pltpu.SemaphoreType.DMA
    out = jax.ShapeDtypeStruct((n_out, n_cen), f32)
    flops = 4 * (HOPS + 1) * n_ex * n_cen * (width + 2 * n_out)
    new_coeffs, residual = pl.pallas_call(
        functools.partial(kernel, cpieces, wpieces, sharpness),
        out_shape=(out, jax.ShapeDtypeStruct((n_out, n_ex), f32)),
        in_specs=[whole, whole, vmem, whole, whole, vmem],
        out_specs=(whole, whole),
        scratch_shapes=[
            pltpu.VMEM((5, n_cen, width), f32),
            pltpu.VMEM((5, n_out, n_cen), f32),
            pltpu.VMEM((n_ex, width), f32),
            pltpu.VMEM((n_out, n_ex), f32),
            pltpu.VMEM((5, n_cen, n_ex), f32),
            pltpu.VMEM((n_out, n_ex), f32),
            pltpu.VMEM((3, n_out, n_cen), f32),
            pltpu.VMEM((2, n_out, n_cen), f32),
        ]
        + [pltpu.VMEM((n_out, n_cen), f32)] * 6
        + [dma((n,))] * 10
        + [dma((nw,))] * 10
        + [dma((4,)), dma((2, nw))],
        compiler_params=pltpu.CompilerParams(
            collective_id=0, has_side_effects=True, vmem_limit_bytes=56 * 2**20
        ),
        cost_estimate=pl.CostEstimate(
            flops=flops, bytes_accessed=7 * 4 * n_out * n_cen, transcendentals=0
        ),
    )(
        examples, targets.T, hop_reach[None, :], centers, coeffs.T,
        (step_size * step_gain)[None, :],
    )
    return (new_coeffs.T, residual.T)


def solution(mesh):
    in_specs = (
        P(("blk", "rep"), None),
        P(("blk", "rep"), None),
        P(("blk", "rep")),
        P("blk", None),
        P("blk", None),
        P("blk"),
    )
    out_specs = (P("blk", None), P(("blk", "rep"), None))
    return jax.shard_map(
        on_device, mesh=mesh, in_specs=in_specs, out_specs=out_specs, check_vma=False
    )
```

```python
import functools
import math

import jax
import jax.numpy as jnp
from jax import lax
from jax.experimental import pallas as pl
from jax.experimental.pallas import tpu as pltpu
from jax.sharding import PartitionSpec as P

HOPS = 4
MESH = pl.DeviceIdType.MESH
OWN, D, X, PY, PX = range(5)
NT = (((1,), (1,)), ((), ()))
NN = (((1,), (0,)), ((), ()))


def spans(sizes):
    out, at = [], 0
    for size in sizes:
        out.append((at, size))
        at += size
    return out


def halves(a):
    hi = a.astype(jnp.bfloat16)
    lo = (a - hi.astype(jnp.float32)).astype(jnp.bfloat16)
    return hi, lo


def product(a, b_hi, b_lo, dims):
    m = a.shape[0]
    a_hi, a_lo = halves(a)
    both = lax.dot_general(
        jnp.concatenate([a_hi, a_lo]), b_hi, dims, preferred_element_type=jnp.float32
    )
    cross = lax.dot_general(a_hi, b_lo, dims, preferred_element_type=jnp.float32)
    return both[:m] + (both[m:] + cross)


def near_share(size):
    return size // 16 * 8


def kernel(
    cpieces, wpieces, sharpness, step_size,
    ex_hbm, tgt_hbm, hop_ref, cen_hbm, cof_hbm, gain_ref,
    newc_hbm, res_hbm,
    cbuf, wbuf, ex, ex2, tgt, kt, res, grad, gsend, rpy, rpx, rx, ry, re, newc,
    d_s, d_r, xa_s, xa_r, xb_s, xb_r, py_s, py_r, px_s, px_r,
    gpy_s, gpy_r, gpx_s, gpx_r, gxa_s, gxa_r, gxb_s, gxb_r, gy_s, gy_r, ge_s, ge_r,
    load_sem, out_sem,
):
    b = lax.axis_index("blk")
    r = lax.axis_index("rep")
    n_blk = lax.axis_size("blk")
    q = lax.rem(b, 4)
    xl = q // 2
    core = lax.rem(q, 2)
    base = b - q
    is_l = xl == 0
    is_h = xl == 1
    up = (lax.rem(b + 4, n_blk), r)
    down = (lax.rem(b + n_blk - 4, n_blk), r)
    near = base + (1 - xl) * 2 + core
    x1 = (near, r)
    x3 = (near, 1 - r)
    x2 = (b, 1 - r)
    peer = (base + xl * 2 + 1 - core, r)

    def load(i, src, dst):
        return pltpu.make_async_copy(src, dst, load_sem.at[i])

    loads = [
        load(0, cen_hbm, cbuf.at[OWN]),
        load(1, cof_hbm, wbuf.at[OWN]),
        load(2, ex_hbm, ex),
        load(3, tgt_hbm, tgt),
    ]
    for copy in loads:
        copy.start()

    barrier = pltpu.get_barrier_semaphore()
    for other in (up, down, x1, x3, x2, peer):
        pl.semaphore_signal(barrier, inc=1, device_id=other, device_id_type=MESH)
    pl.semaphore_wait(barrier, 6)

    nc, nw = len(cpieces), len(wpieces)
    n = nc + nw

    def part(i, slot):
        if i < nc:
            lo, size = cpieces[i]
            return cbuf.at[slot, pl.ds(lo, size)]
        lo, size = wpieces[i - nc]
        return wbuf.at[slot, pl.ds(lo, size)]

    def cut(i):
        if i < nc:
            lo, size = cpieces[i]
            return cbuf, lo, near_share(size), size
        lo, size = wpieces[i - nc]
        return wbuf, lo, near_share(size), size

    def remote(src, dst, ssem, rsem, to):
        return pltpu.make_async_remote_copy(
            src_ref=src, dst_ref=dst, send_sem=ssem, recv_sem=rsem,
            device_id=to, device_id_type=MESH,
        )

    def d_copy(i):
        return remote(part(i, OWN), part(i, D), d_s.at[i], d_r.at[i], up)

    def x_copies(i):
        buf, lo, near_rows, size = cut(i)
        one, two = pl.ds(lo, near_rows), pl.ds(lo + near_rows, size - near_rows)
        return (
            remote(buf.at[xl, one], buf.at[X, one], xa_s.at[i], xa_r.at[i], x1),
            remote(buf.at[xl, two], buf.at[X, two], xb_s.at[i], xb_r.at[i], x3),
        )

    def py_copy(i):
        return remote(part(i, core), part(i, PY), py_s.at[i], py_r.at[i], peer)

    def px_copy(i):
        return remote(part(i, X), part(i, PX), px_s.at[i], px_r.at[i], peer)

    def rows(j):
        lo, size = wpieces[j]
        return pl.ds(lo, size)

    def gpy_copy(j):
        return remote(gsend.at[0, rows(j)], rpy.at[rows(j)], gpy_s.at[j], gpy_r.at[j], peer)

    def gpx_copy(j):
        return remote(gsend.at[1, rows(j)], rpx.at[rows(j)], gpx_s.at[j], gpx_r.at[j], peer)

    def gx_copies(j):
        lo, size = wpieces[j]
        near_rows = near_share(size)
        one, two = pl.ds(lo, near_rows), pl.ds(lo + near_rows, size - near_rows)
        return (
            remote(grad.at[X, one], rx.at[one], gxa_s.at[j], gxa_r.at[j], x1),
            remote(grad.at[X, two], rx.at[two], gxb_s.at[j], gxb_r.at[j], x3),
        )

    def gy_copy(j):
        return remote(grad.at[D, rows(j)], ry.at[rows(j)], gy_s.at[j], gy_r.at[j], down)

    def ge_copy(j):
        return remote(grad.at[OWN, rows(j)], re.at[rows(j)], ge_s.at[j], ge_r.at[j], x2)

    hop_of = {OWN: 0, D: 4, X: 2, PY: 3 - 2 * core, PX: 1 + 2 * core}

    def scores(slot, lo, size):
        products = product(cbuf[slot, lo:lo + size, :], ex2[0], ex2[1], NT)
        visible = (hop_ref[...] > hop_of[slot]).astype(jnp.float32)
        values = jnp.exp(sharpness * products) * visible
        kt[0, slot, lo:lo + size, :], kt[1, slot, lo:lo + size, :] = halves(values)

    def arrive(i):
        d_copy(i).wait_recv()

        @pl.when(is_h)
        def _():
            for copy in x_copies(i):
                copy.start()

        @pl.when(core == 1)
        def _():
            py_copy(i).start()

        d_copy(i).wait_send()
        if i + 3 < n:
            d_copy(i + 3).start()
        if i + nc < n:
            @pl.when(is_l)
            def _():
                for copy in x_copies(i + nc):
                    copy.start()

    def spread(i):
        for copy in x_copies(i):
            copy.wait_recv()
        px_copy(i).start()

    def ready(i):
        py_copy(i).wait_recv()
        px_copy(i).wait_recv()

    def contract(j):
        ready(nc + j)
        lo, size = wpieces[j]
        hi = lo + size
        total = -tgt[lo:hi, :]
        for slot in (OWN, D, X, PY, PX):
            total = total + product(wbuf[slot, lo:hi, :], kt[0, slot], kt[1, slot], NN)
        res[lo:hi, :] = total

        def term(slot):
            return product(res[lo:hi, :], kt[0, slot], kt[1, slot], NT)

        gsend[1, lo:hi, :] = term(PX)
        gpx_copy(j).start()
        gsend[0, lo:hi, :] = term(PY)
        gpy_copy(j).start()
        for slot in (X, D, OWN):
            grad[slot, lo:hi, :] = term(slot)
        out_copy(0, j).start()

    def out_copy(which, j):
        src, dst = ((res, res_hbm), (newc, newc_hbm))[which]
        return pltpu.make_async_copy(src.at[rows(j)], dst.at[rows(j)], out_sem.at[which, j])

    def fold(j):
        lo, size = wpieces[j]
        hi = lo + size
        gpx_copy(j).wait_recv()
        grad[X, lo:hi, :] = grad[X, lo:hi, :] + rpx[lo:hi, :]
        for copy in gx_copies(j):
            copy.start()
        gpy_copy(j).wait_recv()

        @pl.when(core == 0)
        def _():
            grad[OWN, lo:hi, :] = grad[OWN, lo:hi, :] + rpy[lo:hi, :]

        @pl.when(core == 1)
        def _():
            grad[D, lo:hi, :] = grad[D, lo:hi, :] + rpy[lo:hi, :]

        @pl.when(is_l)
        def _():
            gy_copy(j).start()

    def descend(j):
        lo, size = wpieces[j]
        hi = lo + size
        for copy in gx_copies(j):
            copy.wait_recv()

        @pl.when(is_h)
        def _():
            grad[D, lo:hi, :] = grad[D, lo:hi, :] + rx[lo:hi, :]
            gy_copy(j).start()

        @pl.when(is_l)
        def _():
            grad[OWN, lo:hi, :] = grad[OWN, lo:hi, :] + rx[lo:hi, :]

    def home(j):
        lo, size = wpieces[j]
        hi = lo + size
        gy_copy(j).wait_recv()
        grad[OWN, lo:hi, :] = grad[OWN, lo:hi, :] + ry[lo:hi, :]
        ge_copy(j).start()

    def finish(j):
        lo, size = wpieces[j]
        hi = lo + size
        ge_copy(j).wait_recv()
        total = grad[OWN, lo:hi, :] + re[lo:hi, :]
        newc[lo:hi, :] = wbuf[OWN, lo:hi, :] - (step_size * gain_ref[...]) * total
        out_copy(1, j).start()

    loads[0].wait()
    d_copy(0).start()
    d_copy(1).start()
    d_copy(2).start()

    @pl.when(is_l)
    def _():
        for i in range(nc):
            for copy in x_copies(i):
                copy.start()

    loads[1].wait()

    @pl.when(core == 0)
    def _():
        for i in range(n):
            py_copy(i).start()

    loads[2].wait()
    ex2[0], ex2[1] = halves(ex[...])
    scores(OWN, 0, cbuf.shape[1])
    loads[3].wait()

    def in_range(j):
        return 0 <= j < nw

    for i in range(nc):
        arrive(i)
        scores(D, *cpieces[i])
        spread(i)
        ready(i)
        for slot in (X, PY, PX):
            scores(slot, *cpieces[i])
    arrive(nc)
    for j in range(nw + 3):
        if in_range(j):
            spread(nc + j)
        if in_range(j + 1):
            arrive(nc + j + 1)
        if in_range(j):
            contract(j)
        if in_range(j - 1):
            descend(j - 1)
        if in_range(j):
            fold(j)
        if in_range(j - 2):
            home(j - 2)
        if in_range(j - 3):
            finish(j - 3)

    for i in range(n):
        for copy in x_copies(i):
            copy.wait_send()
        py_copy(i).wait_send()
        px_copy(i).wait_send()
    for j in range(nw):
        for copy in gx_copies(j):
            copy.wait_send()
        for make in (gpy_copy, gpx_copy, gy_copy, ge_copy):
            make(j).wait_send()
        out_copy(0, j).wait()
        out_copy(1, j).wait()


def on_device(examples, targets, hop_reach, centers, coeffs, step_gain):
    n_ex, width = examples.shape
    n_cen, n_out = coeffs.shape
    sharpness = 0.5 / math.sqrt(width)
    step_size = 1.0 / math.sqrt(n_ex * lax.axis_size("rep") * (HOPS + 1))
    cpieces = spans([n_cen // 4] * 4)
    wpieces = spans([104,208,208,208,144,128])
    nc, nw = len(cpieces), len(wpieces)
    n = nc + nw
    f32 = jnp.float32
    whole = pl.BlockSpec(memory_space=pl.ANY)
    vmem = pl.BlockSpec(memory_space=pltpu.VMEM)
    dma = pltpu.SemaphoreType.DMA
    out = jax.ShapeDtypeStruct((n_out, n_cen), f32)
    flops = 4 * (HOPS + 1) * n_ex * n_cen * (width + 2 * n_out)
    new_coeffs, residual = pl.pallas_call(
        functools.partial(kernel, cpieces, wpieces, sharpness, step_size),
        out_shape=(out, jax.ShapeDtypeStruct((n_out, n_ex), f32)),
        in_specs=[whole, whole, vmem, whole, whole, vmem],
        out_specs=(whole, whole),
        scratch_shapes=[
            pltpu.VMEM((5, n_cen, width), f32),
            pltpu.VMEM((5, n_out, n_cen), f32),
            pltpu.VMEM((n_ex, width), f32),
            pltpu.VMEM((2, n_ex, width), jnp.bfloat16),
            pltpu.VMEM((n_out, n_ex), f32),
            pltpu.VMEM((2, 5, n_cen, n_ex), jnp.bfloat16),
            pltpu.VMEM((n_out, n_ex), f32),
            pltpu.VMEM((3, n_out, n_cen), f32),
            pltpu.VMEM((2, n_out, n_cen), f32),
        ]
        + [pltpu.VMEM((n_out, n_cen), f32)] * 6
        + [dma((n,))] * 10
        + [dma((nw,))] * 12
        + [dma((4,)), dma((2, nw))],
        compiler_params=pltpu.CompilerParams(
            collective_id=0, has_side_effects=True, vmem_limit_bytes=56 * 2**20
        ),
        cost_estimate=pl.CostEstimate(
            flops=flops, bytes_accessed=7 * 4 * n_out * n_cen, transcendentals=0
        ),
    )(
        examples, targets.T, hop_reach[None, :], centers, coeffs.T, step_gain[None, :],
    )
    return (new_coeffs.T, residual.T)


def solution(mesh):
    in_specs = (
        P(("blk", "rep"), None),
        P(("blk", "rep"), None),
        P(("blk", "rep")),
        P("blk", None),
        P("blk", None),
        P("blk"),
    )
    out_specs = (P("blk", None), P(("blk", "rep"), None))
    return jax.shard_map(
        on_device, mesh=mesh, in_specs=in_specs, out_specs=out_specs, check_vma=False
    )
```

```python
import functools
import math

import jax
import jax.numpy as jnp
from jax import lax
from jax.experimental import pallas as pl
from jax.experimental.pallas import tpu as pltpu
from jax.sharding import PartitionSpec as P

HOPS = 4
MESH = pl.DeviceIdType.MESH
OWN, D, X, PY, PX = range(5)
NT = (((1,), (1,)), ((), ()))
NN = (((1,), (0,)), ((), ()))


def spans(sizes):
    out, at = [], 0
    for size in sizes:
        out.append((at, size))
        at += size
    return out


def halves(a):
    hi = a.astype(jnp.bfloat16)
    lo = (a - hi.astype(jnp.float32)).astype(jnp.bfloat16)
    return hi, lo


def product(a, b_hi, b_lo, dims):
    m = a.shape[0]
    a_hi, a_lo = halves(a)
    both = lax.dot_general(
        jnp.concatenate([a_hi, a_lo]), b_hi, dims, preferred_element_type=jnp.float32
    )
    cross = lax.dot_general(a_hi, b_lo, dims, preferred_element_type=jnp.float32)
    return both[:m] + (both[m:] + cross)


def near_share(size):
    return size // 16 * 8


def kernel(
    cpieces, wpieces, sharpness, step_size,
    ex_hbm, tgt_hbm, hop_ref, cen_hbm, cof_hbm, gain_ref,
    newc_hbm, res_hbm,
    cbuf, wbuf, ex, ex2, tgt, kt, res, grad, gsend, rpy, rpx, rx, ry, re, newc,
    d_s, d_r, e_s, e_r, xa_s, xa_r, xb_s, xb_r, py_s, py_r, px_s, px_r,
    gpy_s, gpy_r, gpx_s, gpx_r, gxa_s, gxa_r, gxb_s, gxb_r, gy_s, gy_r, ge_s, ge_r,
    load_sem, out_sem,
):
    b = lax.axis_index("blk")
    r = lax.axis_index("rep")
    n_blk = lax.axis_size("blk")
    q = lax.rem(b, 4)
    xl = q // 2
    core = lax.rem(q, 2)
    base = b - q
    is_l = xl == 0
    is_h = xl == 1
    up = (lax.rem(b + 4, n_blk), r)
    down = (lax.rem(b + n_blk - 4, n_blk), r)
    near = base + (1 - xl) * 2 + core
    x1 = (near, r)
    x3 = (near, 1 - r)
    x2 = (b, 1 - r)
    peer = (base + xl * 2 + 1 - core, r)

    def load(i, src, dst):
        return pltpu.make_async_copy(src, dst, load_sem.at[i])

    loads = [
        load(0, cen_hbm, cbuf.at[OWN]),
        load(1, cof_hbm, wbuf.at[OWN]),
        load(2, ex_hbm, ex),
        load(3, tgt_hbm, tgt),
    ]
    for copy in loads:
        copy.start()

    barrier = pltpu.get_barrier_semaphore()
    for other in (up, down, x1, x3, x2, peer):
        pl.semaphore_signal(barrier, inc=1, device_id=other, device_id_type=MESH)
    pl.semaphore_wait(barrier, 6)

    nc, nw = len(cpieces), len(wpieces)
    n = nc + nw

    def part(i, slot):
        if i < nc:
            lo, size = cpieces[i]
            return cbuf.at[slot, pl.ds(lo, size)]
        lo, size = wpieces[i - nc]
        return wbuf.at[slot, pl.ds(lo, size)]

    def cut(i):
        if i < nc:
            lo, size = cpieces[i]
            half = pl.ds(lo + size // 2 * r, size // 2)
            return cbuf, half, half
        lo, size = wpieces[i - nc]
        near_rows = near_share(size)
        return wbuf, pl.ds(lo, near_rows), pl.ds(lo + near_rows, size - near_rows)

    def remote(src, dst, ssem, rsem, to):
        return pltpu.make_async_remote_copy(
            src_ref=src, dst_ref=dst, send_sem=ssem, recv_sem=rsem,
            device_id=to, device_id_type=MESH,
        )

    def d_copy(i):
        if i < nc:
            lo, size = cpieces[i]
            span = pl.ds(lo + size // 4 * r, size // 4 * 3)
            return remote(cbuf.at[OWN, span], cbuf.at[D, span], d_s.at[i], d_r.at[i], up)
        return remote(part(i, OWN), part(i, D), d_s.at[i], d_r.at[i], up)

    def e_copy(i):
        lo, size = cpieces[i]
        span = pl.ds(lo + size // 4 * 3 * r, size // 4)
        return remote(cbuf.at[D, span], cbuf.at[D, span], e_s.at[i], e_r.at[i], x2)

    def x_copies(i):
        buf, one, two = cut(i)
        return (
            remote(buf.at[xl, one], buf.at[X, one], xa_s.at[i], xa_r.at[i], x1),
            remote(buf.at[xl, two], buf.at[X, two], xb_s.at[i], xb_r.at[i], x3),
        )

    def py_copy(i):
        return remote(part(i, core), part(i, PY), py_s.at[i], py_r.at[i], peer)

    def px_copy(i):
        return remote(part(i, X), part(i, PX), px_s.at[i], px_r.at[i], peer)

    def rows(j):
        lo, size = wpieces[j]
        return pl.ds(lo, size)

    def gpy_copy(j):
        return remote(gsend.at[0, rows(j)], rpy.at[rows(j)], gpy_s.at[j], gpy_r.at[j], peer)

    def gpx_copy(j):
        return remote(gsend.at[1, rows(j)], rpx.at[rows(j)], gpx_s.at[j], gpx_r.at[j], peer)

    def gx_copies(j):
        lo, size = wpieces[j]
        near_rows = near_share(size)
        one, two = pl.ds(lo, near_rows), pl.ds(lo + near_rows, size - near_rows)
        return (
            remote(grad.at[X, one], rx.at[one], gxa_s.at[j], gxa_r.at[j], x1),
            remote(grad.at[X, two], rx.at[two], gxb_s.at[j], gxb_r.at[j], x3),
        )

    def gy_copy(j):
        return remote(grad.at[D, rows(j)], ry.at[rows(j)], gy_s.at[j], gy_r.at[j], down)

    def ge_copy(j):
        return remote(grad.at[OWN, rows(j)], re.at[rows(j)], ge_s.at[j], ge_r.at[j], x2)

    hop_of = {OWN: 0, D: 4, X: 2, PY: 3 - 2 * core, PX: 1 + 2 * core}

    def scores(slot, lo, size):
        products = product(cbuf[slot, lo:lo + size, :], ex2[0], ex2[1], NT)
        visible = (hop_ref[...] > hop_of[slot]).astype(jnp.float32)
        values = jnp.exp(sharpness * products) * visible
        kt[0, slot, lo:lo + size, :], kt[1, slot, lo:lo + size, :] = halves(values)

    def arrive(i):
        d_copy(i).wait_recv()
        if i < nc:
            e_copy(i).start()

        @pl.when(is_h)
        def _():
            for copy in x_copies(i):
                copy.start()

        if i >= nc:
            complete(i)
        d_copy(i).wait_send()
        if i + 3 < n:
            d_copy(i + 3).start()
        if nc <= i + nc - 1 < n:
            @pl.when(is_l)
            def _():
                for copy in x_copies(i + nc - 1):
                    copy.start()

    def complete(i):
        if i < nc:
            e_copy(i).wait_recv()

        @pl.when(core == 1)
        def _():
            py_copy(i).start()

    def spread(i):
        for copy in x_copies(i):
            copy.wait_recv()
        px_copy(i).start()

    def ready(i):
        py_copy(i).wait_recv()
        px_copy(i).wait_recv()

    def contract(j):
        ready(nc + j)
        lo, size = wpieces[j]
        hi = lo + size
        total = -tgt[lo:hi, :]
        for slot in (OWN, D, X, PY, PX):
            total = total + product(wbuf[slot, lo:hi, :], kt[0, slot], kt[1, slot], NN)
        res[lo:hi, :] = total

        def term(slot):
            return product(res[lo:hi, :], kt[0, slot], kt[1, slot], NT)

        gsend[1, lo:hi, :] = term(PX)
        gpx_copy(j).start()
        gsend[0, lo:hi, :] = term(PY)
        gpy_copy(j).start()
        for slot in (X, D, OWN):
            grad[slot, lo:hi, :] = term(slot)
        out_copy(0, j).start()

    def out_copy(which, j):
        src, dst = ((res, res_hbm), (newc, newc_hbm))[which]
        return pltpu.make_async_copy(src.at[rows(j)], dst.at[rows(j)], out_sem.at[which, j])

    def fold(j):
        lo, size = wpieces[j]
        hi = lo + size
        gpx_copy(j).wait_recv()
        grad[X, lo:hi, :] = grad[X, lo:hi, :] + rpx[lo:hi, :]
        for copy in gx_copies(j):
            copy.start()
        gpy_copy(j).wait_recv()

        @pl.when(core == 0)
        def _():
            grad[OWN, lo:hi, :] = grad[OWN, lo:hi, :] + rpy[lo:hi, :]

        @pl.when(core == 1)
        def _():
            grad[D, lo:hi, :] = grad[D, lo:hi, :] + rpy[lo:hi, :]

        @pl.when(is_l)
        def _():
            gy_copy(j).start()

    def descend(j):
        lo, size = wpieces[j]
        hi = lo + size
        for copy in gx_copies(j):
            copy.wait_recv()

        @pl.when(is_h)
        def _():
            grad[D, lo:hi, :] = grad[D, lo:hi, :] + rx[lo:hi, :]
            gy_copy(j).start()

        @pl.when(is_l)
        def _():
            grad[OWN, lo:hi, :] = grad[OWN, lo:hi, :] + rx[lo:hi, :]

    def home(j):
        lo, size = wpieces[j]
        hi = lo + size
        gy_copy(j).wait_recv()
        grad[OWN, lo:hi, :] = grad[OWN, lo:hi, :] + ry[lo:hi, :]
        ge_copy(j).start()

    def finish(j):
        lo, size = wpieces[j]
        hi = lo + size
        ge_copy(j).wait_recv()
        total = grad[OWN, lo:hi, :] + re[lo:hi, :]
        newc[lo:hi, :] = wbuf[OWN, lo:hi, :] - (step_size * gain_ref[...]) * total
        out_copy(1, j).start()

    loads[0].wait()
    d_copy(0).start()
    d_copy(1).start()
    d_copy(2).start()

    @pl.when(is_l)
    def _():
        for i in range(nc):
            for copy in x_copies(i):
                copy.start()

    loads[1].wait()

    @pl.when(core == 0)
    def _():
        for i in range(n):
            py_copy(i).start()

    loads[2].wait()
    ex2[0], ex2[1] = halves(ex[...])
    scores(OWN, 0, cbuf.shape[1])
    loads[3].wait()

    def in_range(j):
        return 0 <= j < nw

    for i in range(nc + 1):
        if i < nc:
            arrive(i)
        if i > 0:
            complete(i - 1)
            spread(i - 1)
            scores(D, *cpieces[i - 1])
            ready(i - 1)
            for slot in (X, PY, PX):
                scores(slot, *cpieces[i - 1])
    arrive(nc)
    for j in range(nw + 3):
        if in_range(j):
            spread(nc + j)
        if in_range(j + 1):
            arrive(nc + j + 1)
        if in_range(j):
            contract(j)
        if in_range(j - 1):
            descend(j - 1)
        if in_range(j):
            fold(j)
        if in_range(j - 2):
            home(j - 2)
        if in_range(j - 3):
            finish(j - 3)

    for i in range(n):
        if i < nc:
            e_copy(i).wait_send()
        for copy in x_copies(i):
            copy.wait_send()
        py_copy(i).wait_send()
        px_copy(i).wait_send()
    for j in range(nw):
        for copy in gx_copies(j):
            copy.wait_send()
        for make in (gpy_copy, gpx_copy, gy_copy, ge_copy):
            make(j).wait_send()
        out_copy(0, j).wait()
        out_copy(1, j).wait()


def on_device(examples, targets, hop_reach, centers, coeffs, step_gain):
    n_ex, width = examples.shape
    n_cen, n_out = coeffs.shape
    sharpness = 0.5 / math.sqrt(width)
    step_size = 1.0 / math.sqrt(n_ex * lax.axis_size("rep") * (HOPS + 1))
    cpieces = spans([n_cen // 4] * 4)
    wpieces = spans([104,208,208,208,144,128])
    nc, nw = len(cpieces), len(wpieces)
    n = nc + nw
    f32 = jnp.float32
    whole = pl.BlockSpec(memory_space=pl.ANY)
    vmem = pl.BlockSpec(memory_space=pltpu.VMEM)
    dma = pltpu.SemaphoreType.DMA
    out = jax.ShapeDtypeStruct((n_out, n_cen), f32)
    flops = 4 * (HOPS + 1) * n_ex * n_cen * (width + 2 * n_out)
    new_coeffs, residual = pl.pallas_call(
        functools.partial(kernel, cpieces, wpieces, sharpness, step_size),
        out_shape=(out, jax.ShapeDtypeStruct((n_out, n_ex), f32)),
        in_specs=[whole, whole, vmem, whole, whole, vmem],
        out_specs=(whole, whole),
        scratch_shapes=[
            pltpu.VMEM((5, n_cen, width), f32),
            pltpu.VMEM((5, n_out, n_cen), f32),
            pltpu.VMEM((n_ex, width), f32),
            pltpu.VMEM((2, n_ex, width), jnp.bfloat16),
            pltpu.VMEM((n_out, n_ex), f32),
            pltpu.VMEM((2, 5, n_cen, n_ex), jnp.bfloat16),
            pltpu.VMEM((n_out, n_ex), f32),
            pltpu.VMEM((3, n_out, n_cen), f32),
            pltpu.VMEM((2, n_out, n_cen), f32),
        ]
        + [pltpu.VMEM((n_out, n_cen), f32)] * 6
        + [dma((n,))] * 2
        + [dma((nc,))] * 2
        + [dma((n,))] * 8
        + [dma((nw,))] * 12
        + [dma((4,)), dma((2, nw))],
        compiler_params=pltpu.CompilerParams(
            collective_id=0, has_side_effects=True, vmem_limit_bytes=56 * 2**20
        ),
        cost_estimate=pl.CostEstimate(
            flops=flops, bytes_accessed=7 * 4 * n_out * n_cen, transcendentals=0
        ),
    )(
        examples, targets.T, hop_reach[None, :], centers, coeffs.T, step_gain[None, :],
    )
    return (new_coeffs.T, residual.T)


def solution(mesh):
    in_specs = (
        P(("blk", "rep"), None),
        P(("blk", "rep"), None),
        P(("blk", "rep")),
        P("blk", None),
        P("blk", None),
        P("blk"),
    )
    out_specs = (P("blk", None), P(("blk", "rep"), None))
    return jax.shard_map(
        on_device, mesh=mesh, in_specs=in_specs, out_specs=out_specs, check_vma=False
    )
```

```python
import functools
import math

import jax
import jax.numpy as jnp
from jax import lax
from jax.experimental import pallas as pl
from jax.experimental.pallas import tpu as pltpu
from jax.sharding import PartitionSpec as P

HOPS = 4
MESH = pl.DeviceIdType.MESH
OWN, D, X, PY, PX = range(5)
NT = (((1,), (1,)), ((), ()))
NN = (((1,), (0,)), ((), ()))


def spans(sizes):
    out, at = [], 0
    for size in sizes:
        out.append((at, size))
        at += size
    return out


def halves(a):
    hi = a.astype(jnp.bfloat16)
    lo = (a - hi.astype(jnp.float32)).astype(jnp.bfloat16)
    return hi, lo


def product(a, b_hi, b_lo, dims):
    m = a.shape[0]
    a_hi, a_lo = halves(a)
    both = lax.dot_general(
        jnp.concatenate([a_hi, a_lo]), b_hi, dims, preferred_element_type=jnp.float32
    )
    cross = lax.dot_general(a_hi, b_lo, dims, preferred_element_type=jnp.float32)
    return both[:m] + (both[m:] + cross)


def near_share(size):
    return size // 16 * 8


def kernel(
    cpieces, wpieces, sharpness, step_size,
    ex_hbm, tgt_hbm, hop_ref, cen_hbm, cof_hbm, gain_ref,
    newc_hbm, res_hbm,
    cbuf, wbuf, ex, ex2, tgt, kt, res, grad, gsend, rpy, rpx, rx, ry, re, newc,
    d_s, d_r, e_s, e_r, xa_s, xa_r, xb_s, xb_r, py_s, py_r, px_s, px_r,
    gpy_s, gpy_r, gpx_s, gpx_r, gxa_s, gxa_r, gxb_s, gxb_r, gy_s, gy_r, ge_s, ge_r,
    load_sem, out_sem,
):
    b = lax.axis_index("blk")
    r = lax.axis_index("rep")
    n_blk = lax.axis_size("blk")
    q = lax.rem(b, 4)
    xl = q // 2
    core = lax.rem(q, 2)
    base = b - q
    is_l = xl == 0
    is_h = xl == 1
    up = (lax.rem(b + 4, n_blk), r)
    down = (lax.rem(b + n_blk - 4, n_blk), r)
    near = base + (1 - xl) * 2 + core
    x1 = (near, r)
    x3 = (near, 1 - r)
    x2 = (b, 1 - r)
    peer = (base + xl * 2 + 1 - core, r)

    def load(i, src, dst):
        return pltpu.make_async_copy(src, dst, load_sem.at[i])

    loads = [
        load(0, cen_hbm, cbuf.at[OWN]),
        load(1, cof_hbm, wbuf.at[OWN]),
        load(2, ex_hbm, ex),
        load(3, tgt_hbm, tgt),
    ]
    for copy in loads:
        copy.start()

    barrier = pltpu.get_barrier_semaphore()
    for other in (up, down, x1, x3, x2, peer):
        pl.semaphore_signal(barrier, inc=1, device_id=other, device_id_type=MESH)
    pl.semaphore_wait(barrier, 6)

    nc, nw = len(cpieces), len(wpieces)
    n = nc + nw

    def part(i, slot):
        if i < nc:
            lo, size = cpieces[i]
            return cbuf.at[slot, pl.ds(lo, size)]
        lo, size = wpieces[i - nc]
        return wbuf.at[slot, pl.ds(lo, size)]

    def cut(i):
        if i < nc:
            lo, size = cpieces[i]
            half = pl.ds(lo + size // 2 * r, size // 2)
            return cbuf, half, half
        lo, size = wpieces[i - nc]
        near_rows = near_share(size)
        return wbuf, pl.ds(lo, near_rows), pl.ds(lo + near_rows, size - near_rows)

    def remote(src, dst, ssem, rsem, to):
        return pltpu.make_async_remote_copy(
            src_ref=src, dst_ref=dst, send_sem=ssem, recv_sem=rsem,
            device_id=to, device_id_type=MESH,
        )

    def d_copy(i):
        if i < nc:
            lo, size = cpieces[i]
            span = pl.ds(lo + size // 8 * 3 * r, size // 8 * 5)
            return remote(cbuf.at[OWN, span], cbuf.at[D, span], d_s.at[i], d_r.at[i], up)
        return remote(part(i, OWN), part(i, D), d_s.at[i], d_r.at[i], up)

    def e_copy(i):
        lo, size = cpieces[i]
        span = pl.ds(lo + size // 8 * 5 * r, size // 8 * 3)
        return remote(cbuf.at[D, span], cbuf.at[D, span], e_s.at[i], e_r.at[i], x2)

    def x_copies(i):
        buf, one, two = cut(i)
        return (
            remote(buf.at[xl, one], buf.at[X, one], xa_s.at[i], xa_r.at[i], x1),
            remote(buf.at[xl, two], buf.at[X, two], xb_s.at[i], xb_r.at[i], x3),
        )

    def py_copy(i):
        return remote(part(i, core), part(i, PY), py_s.at[i], py_r.at[i], peer)

    def px_copy(i):
        return remote(part(i, X), part(i, PX), px_s.at[i], px_r.at[i], peer)

    def rows(j):
        lo, size = wpieces[j]
        return pl.ds(lo, size)

    def gpy_copy(j):
        return remote(gsend.at[0, rows(j)], rpy.at[rows(j)], gpy_s.at[j], gpy_r.at[j], peer)

    def gpx_copy(j):
        return remote(gsend.at[1, rows(j)], rpx.at[rows(j)], gpx_s.at[j], gpx_r.at[j], peer)

    def gx_copies(j):
        lo, size = wpieces[j]
        near_rows = near_share(size)
        one, two = pl.ds(lo, near_rows), pl.ds(lo + near_rows, size - near_rows)
        return (
            remote(grad.at[X, one], rx.at[one], gxa_s.at[j], gxa_r.at[j], x1),
            remote(grad.at[X, two], rx.at[two], gxb_s.at[j], gxb_r.at[j], x3),
        )

    def gy_copy(j):
        return remote(grad.at[D, rows(j)], ry.at[rows(j)], gy_s.at[j], gy_r.at[j], down)

    def ge_copy(j):
        return remote(grad.at[OWN, rows(j)], re.at[rows(j)], ge_s.at[j], ge_r.at[j], x2)

    hop_of = {OWN: 0, D: 4, X: 2, PY: 3 - 2 * core, PX: 1 + 2 * core}

    def scores(slot, lo, size):
        products = product(cbuf[slot, lo:lo + size, :], ex2[0], ex2[1], NT)
        visible = (hop_ref[...] > hop_of[slot]).astype(jnp.float32)
        values = jnp.exp(sharpness * products) * visible
        kt[0, slot, lo:lo + size, :], kt[1, slot, lo:lo + size, :] = halves(values)

    def arrive(i):
        d_copy(i).wait_recv()
        if i < nc:
            e_copy(i).start()

        @pl.when(is_h)
        def _():
            for copy in x_copies(i):
                copy.start()

        if i >= nc:
            complete(i)
        d_copy(i).wait_send()
        if i + 4 < n:
            d_copy(i + 4).start()
        if nc <= i + nc - 1 < n:
            @pl.when(is_l)
            def _():
                for copy in x_copies(i + nc - 1):
                    copy.start()

    def complete(i):
        if i < nc:
            e_copy(i).wait_recv()

        @pl.when(core == 1)
        def _():
            py_copy(i).start()

    def spread(i):
        for copy in x_copies(i):
            copy.wait_recv()
        px_copy(i).start()

    def ready(i):
        py_copy(i).wait_recv()
        px_copy(i).wait_recv()

    def contract(j):
        ready(nc + j)
        lo, size = wpieces[j]
        hi = lo + size
        total = -tgt[lo:hi, :]
        for slot in (OWN, D, X, PY, PX):
            total = total + product(wbuf[slot, lo:hi, :], kt[0, slot], kt[1, slot], NN)
        res[lo:hi, :] = total

        def term(slot):
            return product(res[lo:hi, :], kt[0, slot], kt[1, slot], NT)

        gsend[1, lo:hi, :] = term(PX)
        gpx_copy(j).start()
        gsend[0, lo:hi, :] = term(PY)
        gpy_copy(j).start()
        for slot in (X, D, OWN):
            grad[slot, lo:hi, :] = term(slot)
        out_copy(0, j).start()

    def out_copy(which, j):
        src, dst = ((res, res_hbm), (newc, newc_hbm))[which]
        return pltpu.make_async_copy(src.at[rows(j)], dst.at[rows(j)], out_sem.at[which, j])

    def fold(j):
        lo, size = wpieces[j]
        hi = lo + size
        gpx_copy(j).wait_recv()
        grad[X, lo:hi, :] = grad[X, lo:hi, :] + rpx[lo:hi, :]
        for copy in gx_copies(j):
            copy.start()
        gpy_copy(j).wait_recv()

        @pl.when(core == 0)
        def _():
            grad[OWN, lo:hi, :] = grad[OWN, lo:hi, :] + rpy[lo:hi, :]

        @pl.when(core == 1)
        def _():
            grad[D, lo:hi, :] = grad[D, lo:hi, :] + rpy[lo:hi, :]

        @pl.when(is_l)
        def _():
            gy_copy(j).start()

    def descend(j):
        lo, size = wpieces[j]
        hi = lo + size
        for copy in gx_copies(j):
            copy.wait_recv()

        @pl.when(is_h)
        def _():
            grad[D, lo:hi, :] = grad[D, lo:hi, :] + rx[lo:hi, :]
            gy_copy(j).start()

        @pl.when(is_l)
        def _():
            grad[OWN, lo:hi, :] = grad[OWN, lo:hi, :] + rx[lo:hi, :]

    def home(j):
        lo, size = wpieces[j]
        hi = lo + size
        gy_copy(j).wait_recv()
        grad[OWN, lo:hi, :] = grad[OWN, lo:hi, :] + ry[lo:hi, :]
        ge_copy(j).start()

    def finish(j):
        lo, size = wpieces[j]
        hi = lo + size
        ge_copy(j).wait_recv()
        total = grad[OWN, lo:hi, :] + re[lo:hi, :]
        newc[lo:hi, :] = wbuf[OWN, lo:hi, :] - (step_size * gain_ref[...]) * total
        out_copy(1, j).start()

    loads[0].wait()
    d_copy(0).start()
    d_copy(1).start()
    d_copy(2).start()
    d_copy(3).start()

    @pl.when(is_l)
    def _():
        for i in range(nc):
            for copy in x_copies(i):
                copy.start()

    loads[1].wait()

    @pl.when(core == 0)
    def _():
        for i in range(n):
            py_copy(i).start()

    loads[2].wait()
    ex2[0], ex2[1] = halves(ex[...])
    scores(OWN, 0, cbuf.shape[1])
    loads[3].wait()

    def in_range(j):
        return 0 <= j < nw

    for i in range(nc + 1):
        if i < nc:
            arrive(i)
        if i > 0:
            complete(i - 1)
            spread(i - 1)
            scores(D, *cpieces[i - 1])
            ready(i - 1)
            for slot in (X, PY, PX):
                scores(slot, *cpieces[i - 1])
    arrive(nc)
    for j in range(nw + 3):
        if in_range(j):
            spread(nc + j)
        if in_range(j + 1):
            arrive(nc + j + 1)
        if in_range(j):
            contract(j)
        if in_range(j - 1):
            descend(j - 1)
        if in_range(j):
            fold(j)
        if in_range(j - 2):
            home(j - 2)
        if in_range(j - 3):
            finish(j - 3)

    for i in range(n):
        if i < nc:
            e_copy(i).wait_send()
        for copy in x_copies(i):
            copy.wait_send()
        py_copy(i).wait_send()
        px_copy(i).wait_send()
    for j in range(nw):
        for copy in gx_copies(j):
            copy.wait_send()
        for make in (gpy_copy, gpx_copy, gy_copy, ge_copy):
            make(j).wait_send()
        out_copy(0, j).wait()
        out_copy(1, j).wait()


def on_device(examples, targets, hop_reach, centers, coeffs, step_gain):
    n_ex, width = examples.shape
    n_cen, n_out = coeffs.shape
    sharpness = 0.5 / math.sqrt(width)
    step_size = 1.0 / math.sqrt(n_ex * lax.axis_size("rep") * (HOPS + 1))
    cpieces = spans([n_cen // 4] * 4)
    wpieces = spans([104,208,208,208,144,128])
    nc, nw = len(cpieces), len(wpieces)
    n = nc + nw
    f32 = jnp.float32
    whole = pl.BlockSpec(memory_space=pl.ANY)
    vmem = pl.BlockSpec(memory_space=pltpu.VMEM)
    dma = pltpu.SemaphoreType.DMA
    out = jax.ShapeDtypeStruct((n_out, n_cen), f32)
    flops = 4 * (HOPS + 1) * n_ex * n_cen * (width + 2 * n_out)
    new_coeffs, residual = pl.pallas_call(
        functools.partial(kernel, cpieces, wpieces, sharpness, step_size),
        out_shape=(out, jax.ShapeDtypeStruct((n_out, n_ex), f32)),
        in_specs=[whole, whole, vmem, whole, whole, vmem],
        out_specs=(whole, whole),
        scratch_shapes=[
            pltpu.VMEM((5, n_cen, width), f32),
            pltpu.VMEM((5, n_out, n_cen), f32),
            pltpu.VMEM((n_ex, width), f32),
            pltpu.VMEM((2, n_ex, width), jnp.bfloat16),
            pltpu.VMEM((n_out, n_ex), f32),
            pltpu.VMEM((2, 5, n_cen, n_ex), jnp.bfloat16),
            pltpu.VMEM((n_out, n_ex), f32),
            pltpu.VMEM((3, n_out, n_cen), f32),
            pltpu.VMEM((2, n_out, n_cen), f32),
        ]
        + [pltpu.VMEM((n_out, n_cen), f32)] * 6
        + [dma((n,))] * 2
        + [dma((nc,))] * 2
        + [dma((n,))] * 8
        + [dma((nw,))] * 12
        + [dma((4,)), dma((2, nw))],
        compiler_params=pltpu.CompilerParams(
            collective_id=0, has_side_effects=True, vmem_limit_bytes=56 * 2**20
        ),
        cost_estimate=pl.CostEstimate(
            flops=flops, bytes_accessed=7 * 4 * n_out * n_cen, transcendentals=0
        ),
    )(
        examples, targets.T, hop_reach[None, :], centers, coeffs.T, step_gain[None, :],
    )
    return (new_coeffs.T, residual.T)


def solution(mesh):
    in_specs = (
        P(("blk", "rep"), None),
        P(("blk", "rep"), None),
        P(("blk", "rep")),
        P("blk", None),
        P("blk", None),
        P("blk"),
    )
    out_specs = (P("blk", None), P(("blk", "rep"), None))
    return jax.shard_map(
        on_device, mesh=mesh, in_specs=in_specs, out_specs=out_specs, check_vma=False
    )
```
